512 devices in a mesh: dom: 16 (over z_lo, core), rep: 32 (over x, z_hi, y).
Axes of the slice: x: 4, y: 4, z: 16 (z_hi: 2, z_lo: 8; z = z_hi * 8 + z_lo), core: 2. Of those that a mesh axis runs over, the one named last changes fastest.
Arguments:
- cells: int32 [3, 8388608], P(None, ('dom', 'rep')), may hold values from 0 to 191, as said below
- offsets: float32 [3, 8388608], P(None, ('dom', 'rep')), may hold values from 0 to 1
- displacements: float32 [3, 8388608], P(None, ('dom', 'rep')), may hold values from -1 to 1
- block_split: int32 [262144], P(('dom', 'rep')), may hold values from 8 to 24
- fields: float32 [2, 32, 36864], P(None, 'dom'), may hold values from -12 to 12
- crossing: int32 [512, 2, 16], P(('dom', 'rep')), may hold values from 0 to 511, as said below
- crossing_counts: int32 [512, 2], P(('dom', 'rep')), may hold values from 0 to 16, as said below
Outputs:
- new_offsets: float32 [3, 8388608], P(None, ('dom', 'rep'))
- density: float32 [2, 32, 36864], P(None, 'dom', 'rep')
- arrivals: float32 [2, 3, 262144], P(None, None, ('dom', 'rep'))
The draws below stay inside these ranges and needn't reach their ends.
Inputs may be any that keep to these rules, and one draw needn't show every extreme that they name: x and y cells 0 to 191, z the layer 0 to 1 within the bead's domain; consecutive beads of a chain lie at most one cell apart along each direction (x and y periodically). `crossing`: the 32 entries of one device are distinct chain indices of that device. `crossing_counts`: the used slots are the first ones.
All inputs are finite; a program needn't handle non-finite values.
Results may differ from the reference program's by a relative error of at most 0.0003.
Values sent between devices are 32-bit elements; how exact they have to be, the bound alone decides.
No kernel may reach another device: no remote copies, remote signals or barrier semaphores. Data moves between devices by JAX's collectives and lax.ppermute only.
A program may use at most 192 MiB of HBM per device.

```python
import jax
import jax.numpy as jnp
from jax import lax

GRID = 192
LZ = 2
NB = 32
CH_DEV = 512
MIG = 16
NZ = 32
CHAINS = 262144
BEADS = 8388608
N_DOM = 16
N_REP = 32


def draw_cells(key, part):
    key = jax.random.fold_in(key, 11)
    devices = N_DOM * N_REP
    anchor_key, stride_key = jax.random.split(key)
    limits = jnp.array([GRID, GRID, LZ], jnp.int32).reshape(3, 1, 1, 1)
    anchor = jax.random.randint(anchor_key, (3, devices, 1, CH_DEV), 0, 1 << 20) % limits
    strides = jax.random.randint(stride_key, (3, devices, NB - 1, CH_DEV), -1, 2)
    walked = anchor + jnp.concatenate([jnp.zeros((3, devices, 1, CH_DEV), jnp.int32), jnp.cumsum(strides, axis=2)], axis=2)
    plane_cells = walked[:2] % GRID
    depth_cells = jnp.clip(walked[2:], 0, LZ - 1)
    return jnp.concatenate([plane_cells, depth_cells], axis=0).reshape(3, -1).astype(jnp.int32)


def draw_crossing(key, part):
    key = jax.random.fold_in(key, 37)
    device_keys = jax.random.split(key, N_DOM * N_REP)
    picks = jax.vmap(lambda device_key: jax.random.permutation(device_key, CH_DEV)[:2 * MIG])(device_keys)
    return picks.reshape(-1, 2, MIG).astype(jnp.int32)


def draw_crossing_counts(key, part):
    key = jax.random.fold_in(key, 23)
    slot_total = N_DOM * N_REP * 2
    value_key, first_key, second_key = jax.random.split(key, 3)
    values = jax.random.randint(value_key, (slot_total,), 0, MIG + 1)
    first = jax.random.randint(first_key, (), 0, slot_total)
    second = (first + 1 + jax.random.randint(second_key, (), 0, slot_total - 1)) % slot_total
    values = values.at[first].set(MIG).at[second].set(0)
    return values.reshape(-1, 2).astype(jnp.int32)


def place_ends(entries, stream_key, low, largest):
    longest = entries.shape.index(max(entries.shape))
    spots = []
    for shift in (0, 1):
        where = [jax.random.randint(jax.random.fold_in(stream_key, axis), (), 0, length) for axis, length in enumerate(entries.shape)]
        where[longest] = (where[longest] + shift) % entries.shape[longest]
        spots.append(tuple(where))
    return entries.at[spots[0]].set(low).at[spots[1]].set(largest)


def block_scale(stream_key, dims, cuts, low, top_value):
    loudness, own = 1.0, jax.random.fold_in(stream_key, 6)
    for dim, parts in cuts:
        draws = jnp.exp(jax.random.uniform(jax.random.fold_in(own, dim), (parts,), jnp.float32, low / len(cuts), top_value / len(cuts)))
        loudness = loudness * jnp.repeat(draws, dims[dim] // parts).reshape([-1 if axis == dim else 1 for axis in range(len(dims))])
    return loudness


def normal_values(stream_key, dims, spread, bound, pieces=(), held_as=jnp.bfloat16):
    result = spread * jax.random.normal(stream_key, dims, jnp.float32)
    if pieces:
        result = result * block_scale(stream_key, dims, pieces, -0.22, 0.18)
    return jnp.clip(result, -bound, bound).astype(held_as)


def setup_inputs(seed: int = 0) -> dict:
    key_of = jax.random.split(jax.random.key(seed), 8)
    return {
        "cells": draw_cells(jax.random.fold_in(key_of[7], 71), 0),
        "offsets": jnp.clip(1.0 * jax.random.uniform(key_of[1], (3, BEADS), jnp.float32) ** block_scale(key_of[1], (3, BEADS), ((1, 512),), -0.2, 0.2), 0.0, 1.0),
        "displacements": normal_values(key_of[2], (3, BEADS), 0.2, 1.0, ((1, 512),), jnp.float32),
        "block_split": place_ends(jax.random.randint(key_of[3], (CHAINS,), NB // 4, 3 * NB // 4 + 1), jax.random.fold_in(key_of[3], 1), NB // 4, (3 * NB // 4 + 1) - 1).astype(jnp.int32),
        "fields": normal_values(key_of[4], (2, NZ, GRID * GRID), 2.0, 12.0, ((1, 16),), jnp.float32),
        "crossing": draw_crossing(jax.random.fold_in(key_of[7], 71), 0),
        "crossing_counts": draw_crossing_counts(jax.random.fold_in(key_of[7], 71), 0),
    }


MOBILITY = 0.1


def wrap_gap(stride_gap, period):
    return (stride_gap + period // 2) % period - period // 2


def bond_force(cell_rows, offset_rows):
    stride_gap = cell_rows[:, 1:] - cell_rows[:, :-1]
    plane_gap = wrap_gap(stride_gap[:2], GRID)
    stride_gap = jnp.concatenate([plane_gap, stride_gap[2:]], axis=0).astype(jnp.float32)
    stride_gap = stride_gap + (offset_rows[:, 1:] - offset_rows[:, :-1])
    zeros_row = jnp.zeros_like(stride_gap[:, :1])
    return jnp.concatenate([stride_gap, zeros_row], axis=1) - jnp.concatenate([zeros_row, stride_gap], axis=1)


def field_forces(padded):
    interior = padded[:, 1:-1]
    layer_count = interior.shape[1]
    force_z = (padded[:, :-2] - padded[:, 2:]) * 0.5
    square = interior.reshape(2, layer_count, GRID, GRID)
    force_x = ((jnp.roll(square, 1, 2) - jnp.roll(square, -1, 2)) * 0.5).reshape(2, layer_count, GRID * GRID)
    force_y = ((jnp.roll(square, 1, 3) - jnp.roll(square, -1, 3)) * 0.5).reshape(2, layer_count, GRID * GRID)
    return jnp.stack([force_x, force_y, force_z]).reshape(3, -1)


def move_beads(cell_rows, offset_rows, displace_rows, split_rows, forces, layer_base, layer_count):
    bead_count = cell_rows.shape[1]
    positions_along = jnp.arange(bead_count, dtype=jnp.int32)[:, None]
    species = (positions_along >= split_rows[None, :]).astype(jnp.int32)
    plane_index = cell_rows[0] * GRID + cell_rows[1]
    layer_of = cell_rows[2] + layer_base
    lookup = species * (layer_count * GRID * GRID) + layer_of * (GRID * GRID) + plane_index
    field_push = forces[:, lookup]
    shifted = offset_rows + MOBILITY * (bond_force(cell_rows, offset_rows) + field_push) + displace_rows
    return shifted, species, plane_index, layer_of


def deposit(shifted, species, plane_index, layer_of, upper_layer, layer_count):
    upper_share = jnp.clip(shifted[2], 0.0, 1.0)
    base_index = species * (layer_count * GRID * GRID) + plane_index
    lower_index = (base_index + layer_of * (GRID * GRID)).reshape(-1)
    upper_index = (base_index + upper_layer * (GRID * GRID)).reshape(-1)
    all_index = jnp.concatenate([lower_index, upper_index])
    all_weight = jnp.concatenate([(1.0 - upper_share).reshape(-1), upper_share.reshape(-1)])
    grid_sum = jnp.zeros((2 * layer_count * GRID * GRID,), jnp.float32)
    return grid_sum.at[all_index].add(all_weight)


def crossing_rows(cell_rows, shifted, chosen, count_used, lift_by):
    position = cell_rows.astype(jnp.float32) + shifted
    picked = jnp.take(position, chosen, axis=2)
    picked = picked.at[2].add(lift_by)
    kept_mask = (jnp.arange(chosen.shape[0], dtype=jnp.int32) < count_used).astype(jnp.float32)
    return (picked * kept_mask).reshape(3, -1)


def reference(cells, offsets, displacements, block_split, fields, crossing, crossing_counts):
    devices = N_DOM * N_REP
    layers_all = LZ * N_DOM

    def per_device(array):
        return jnp.moveaxis(array.reshape(3, devices, NB, CH_DEV), 1, 0)

    padded = jnp.concatenate([fields[:, -1:], fields, fields[:, :1]], axis=1)
    forces = field_forces(padded)

    def one_device(density_sum, slices_in):
        cell_rows, offset_rows, displace_rows, split_rows, chosen, count_pair, device_number = slices_in
        layer_base = (device_number // N_REP) * LZ
        shifted, species, plane_index, layer_of = move_beads(cell_rows, offset_rows, displace_rows, split_rows, forces, layer_base, layers_all)
        density_sum = density_sum + deposit(shifted, species, plane_index, layer_of, (layer_of + 1) % layers_all, layers_all)
        rising = crossing_rows(cell_rows, shifted, chosen[0], count_pair[0], -float(LZ))
        falling = crossing_rows(cell_rows, shifted, chosen[1], count_pair[1], float(LZ))
        return density_sum, (shifted.reshape(3, -1), rising, falling)

    slices_all = (per_device(cells), per_device(offsets), per_device(displacements), block_split.reshape(devices, CH_DEV), crossing, crossing_counts, jnp.arange(devices, dtype=jnp.int32))
    start_sum = jnp.zeros((2 * layers_all * GRID * GRID,), jnp.float32)
    density_sum, outputs = lax.scan(one_device, start_sum, slices_all)
    shifted_all, rising, falling = outputs
    density_scale = GRID * GRID * LZ / (N_REP * CH_DEV * NB)
    density = density_sum.reshape(2, layers_all, GRID * GRID) * density_scale
    new_offsets = jnp.moveaxis(shifted_all, 0, 1).reshape(3, -1)
    slot_size = rising.shape[-1]
    rising = jnp.roll(rising.reshape(N_DOM, N_REP, 3, slot_size), 1, 0).reshape(devices, 3, slot_size)
    falling = jnp.roll(falling.reshape(N_DOM, N_REP, 3, slot_size), -1, 0).reshape(devices, 3, slot_size)
    arrivals = jnp.moveaxis(jnp.stack([rising, falling]), 1, 2).reshape(2, 3, -1)
    return new_offsets, density, arrivals
```

```python
import functools

import jax
import jax.numpy as jnp
from jax import lax
from jax.experimental import pallas as pl
from jax.experimental.pallas import tpu as pltpu
from jax.sharding import PartitionSpec as P

GRID = 192
MOBILITY = 0.1
HEAD_BEADS = 8
TAIL_BEAD = 24


def split_two(value):
    high = value.astype(jnp.bfloat16)
    low = (value - high.astype(jnp.float32)).astype(jnp.bfloat16)
    return high, low


def split_three(value):
    high, rest = value.astype(jnp.bfloat16), None
    rest = value - high.astype(jnp.float32)
    mid = rest.astype(jnp.bfloat16)
    low = (rest - mid.astype(jnp.float32)).astype(jnp.bfloat16)
    return high, mid, low


def wrap_gap(gap):
    gap = jnp.where(gap >= GRID // 2, gap - GRID, gap)
    return jnp.where(gap < -(GRID // 2), gap + GRID, gap)


def table_rows(field_ref, below_ref, above_ref, layers):
    parts = [[], [], []]
    for species in range(2):
        planes = [field_ref[species, layer] for layer in range(layers)]
        stack = [below_ref[species]] + planes + [above_ref[species]]
        for layer in range(layers):
            plane = planes[layer]
            back_x = jnp.concatenate([plane[-1:], plane[:-1]], axis=0)
            fore_x = jnp.concatenate([plane[1:], plane[:1]], axis=0)
            back_y = jnp.concatenate([plane[:, -1:], plane[:, :-1]], axis=1)
            fore_y = jnp.concatenate([plane[:, 1:], plane[:, :1]], axis=1)
            parts[0].append((back_x - fore_x) * 0.5)
            parts[1].append((back_y - fore_y) * 0.5)
            parts[2].append((stack[layer] - stack[layer + 2]) * 0.5)
    return [jnp.concatenate(part, axis=1) for part in parts]


def step_kernel(
    layers, beads, chains, cells_ref, offsets_ref, displace_ref, split_ref, field_ref, below_ref,
    above_ref, chosen_ref, used_ref, new_ref, sums_ref, carry_ref, picked_ref,
    table_ref, hot_ref, weight_ref, total_ref, place_ref,
):
    group = hot_ref.shape[1] // chains
    width = 2 * layers * GRID
    half = layers * GRID
    for k, table in enumerate(table_rows(field_ref, below_ref, above_ref, layers)):
        high, low = split_two(table)
        table_ref[k * GRID:(k + 1) * GRID, :] = high
        table_ref[(3 + k) * GRID:(4 + k) * GRID, :] = low
    total_ref[...] = jnp.zeros_like(total_ref)

    def one_bead(j, slot, first, size):
        def row(ref, k, bead):
            return ref[k:k + 1, pl.ds(pl.multiple_of(bead * chains, chains), chains)]

        before = jnp.maximum(j - 1, 0)
        after = jnp.minimum(j + 1, beads - 1)
        x, y, z = (row(cells_ref, k, j) for k in range(3))
        key = z * GRID + y
        if size == width:
            key = key + jnp.where(j >= split_ref[...], half, 0)
        hot = lax.broadcasted_iota(jnp.int32, (size, chains), 0) == key
        hot = jnp.where(hot, 1.0, 0.0).astype(jnp.bfloat16)
        lanes = slice(slot * chains, (slot + 1) * chains)
        hot_ref[0:size, lanes] = hot
        rows = jnp.dot(table_ref[:, first:first + size], hot, preferred_element_type=jnp.float32)
        mask = lax.broadcasted_iota(jnp.int32, (GRID, chains), 0) == x
        moved = []
        for k in range(3):
            pair = rows[k * GRID:(k + 1) * GRID] + rows[(3 + k) * GRID:(4 + k) * GRID]
            push = jnp.sum(jnp.where(mask, pair, 0.0), axis=0, keepdims=True)
            cell, off = row(cells_ref, k, j), row(offsets_ref, k, j)
            gap_after = row(cells_ref, k, after) - cell
            gap_before = cell - row(cells_ref, k, before)
            if k < 2:
                gap_after, gap_before = wrap_gap(gap_after), wrap_gap(gap_before)
            gap_after = gap_after.astype(jnp.float32) + (row(offsets_ref, k, after) - off)
            gap_before = gap_before.astype(jnp.float32) + (off - row(offsets_ref, k, before))
            bond = gap_after - gap_before
            new = off + MOBILITY * (bond + push) + row(displace_ref, k, j)
            new_ref[k:k + 1, pl.ds(pl.multiple_of(j * chains, chains), chains)] = new
            place_ref[k, pl.ds(j, 1), :] = cell.astype(jnp.float32) + new
            moved.append(new)
        share = jnp.clip(moved[2], 0.0, 1.0)
        high, low = split_two(share)
        weight_ref[0:GRID, lanes] = jnp.where(mask, 1.0, 0.0).astype(jnp.bfloat16)
        weight_ref[GRID:2 * GRID, lanes] = jnp.where(
            mask, high.astype(jnp.float32), 0.0).astype(jnp.bfloat16)
        weight_ref[2 * GRID:, lanes] = jnp.where(
            mask, low.astype(jnp.float32), 0.0).astype(jnp.bfloat16)

    def one_group(g, first, size):
        for slot in range(group):
            one_bead(g * group + slot, slot, first, size)
        total_ref[:, first:first + size] += lax.dot_general(
            weight_ref[...], hot_ref[0:size, :], (((1,), (1,)), ((), ())),
            preferred_element_type=jnp.float32)

    pl.loop(0, HEAD_BEADS // group)(lambda g: one_group(g, 0, half))
    pl.loop(HEAD_BEADS // group, TAIL_BEAD // group)(lambda g: one_group(g, 0, width))
    pl.loop(TAIL_BEAD // group, beads // group)(lambda g: one_group(g, half, half))

    for species in range(2):
        base = species * half
        upper = None
        for layer in range(layers):
            lanes = slice(base + layer * GRID, base + (layer + 1) * GRID)
            count = total_ref[0:GRID, lanes]
            rise = total_ref[GRID:2 * GRID, lanes] + total_ref[2 * GRID:, lanes]
            lower = count - rise
            sums_ref[species, layer] = lower if upper is None else lower + upper
            upper = rise
        carry_ref[species] = upper

    slots = chosen_ref.shape[1]
    place = jnp.concatenate([place_ref[k] for k in range(3)], axis=0)
    pieces = jnp.concatenate(split_three(place), axis=0)
    bead_of = lax.broadcasted_iota(jnp.int32, (beads, slots), 1) // (slots // beads)
    own = bead_of == lax.broadcasted_iota(jnp.int32, (beads, slots), 0)
    slot_of = lax.broadcasted_iota(jnp.int32, (1, slots), 1) % (slots // beads)
    for way, lift in ((0, -float(layers)), (1, float(layers))):
        hot = lax.broadcasted_iota(jnp.int32, (chains, slots), 0) == chosen_ref[way:way + 1]
        hot = jnp.where(hot, 1.0, 0.0).astype(jnp.bfloat16)
        got = jnp.dot(pieces, hot, preferred_element_type=jnp.float32)
        kept = slot_of < used_ref[way:way + 1]
        for k in range(3):
            part = sum(
                got[(p * 3 + k) * beads:(p * 3 + k + 1) * beads] for p in range(3))
            line = jnp.sum(jnp.where(own, part, 0.0), axis=0, keepdims=True)
            if k == 2:
                line = line + lift
            picked_ref[way, k:k + 1, :] = jnp.where(kept, line, 0.0)


def bead_step(cells, offsets, displacements, block_split, fields, below, above, chosen, used):
    chains = block_split.shape[1]
    beads = cells.shape[1] // chains
    layers = fields.shape[1]
    width = 2 * layers * GRID
    group = 4
    f32 = jnp.float32
    return pl.pallas_call(
        functools.partial(step_kernel, layers, beads, chains),
        out_shape=(
            jax.ShapeDtypeStruct(offsets.shape, f32),
            jax.ShapeDtypeStruct((2, layers, GRID, GRID), f32),
            jax.ShapeDtypeStruct((2, GRID, GRID), f32),
            jax.ShapeDtypeStruct((2, 3, chosen.shape[1]), f32),
        ),
        in_specs=[pl.BlockSpec(memory_space=pltpu.VMEM)] * 9,
        out_specs=[pl.BlockSpec(memory_space=pltpu.VMEM)] * 4,
        scratch_shapes=[
            pltpu.VMEM((6 * GRID, width), jnp.bfloat16),
            pltpu.VMEM((width, group * chains), jnp.bfloat16),
            pltpu.VMEM((3 * GRID, group * chains), jnp.bfloat16),
            pltpu.VMEM((3 * GRID, width), f32),
            pltpu.VMEM((3, beads, chains), f32),
        ],
        compiler_params=pltpu.CompilerParams(vmem_limit_bytes=48 * 1024 * 1024),
        name="bead_step",
    )(cells, offsets, displacements, block_split, fields, below, above, chosen, used)


def shifted(value, axis, steps):
    count = lax.axis_size(axis)
    return lax.ppermute(value, axis, [(i, (i + steps) % count) for i in range(count)])


def shards(cells, offsets, displacements, block_split, fields, crossing, crossing_counts):
    chain_count = block_split.shape[0]
    bead_count = cells.shape[1] // chain_count
    layer_count = fields.shape[1]
    planes = fields.reshape(2, layer_count, GRID, GRID)
    below = shifted(planes[:, -1], "dom", 1)
    above = shifted(planes[:, 0], "dom", -1)
    chosen = jnp.tile(crossing[0], (1, bead_count))
    used = jnp.broadcast_to(crossing_counts[0][:, None], chosen.shape)
    new, sums, carry, picked = bead_step(
        cells, offsets, displacements, block_split[None], planes, below, above, chosen, used)
    carried = shifted(carry, "dom", 1)
    arrived = jnp.stack([shifted(picked[0], "dom", 1), shifted(picked[1], "dom", -1)])
    sums = sums.at[:, 0].add(carried)
    density_sum = lax.psum_scatter(
        sums.reshape(2, layer_count, -1), "rep", scatter_dimension=2, tiled=True)
    density_scale = GRID * GRID * layer_count / (lax.axis_size("rep") * chain_count * bead_count)
    return new, density_sum * density_scale, arrived


def solution(mesh):
    in_specs = (
        P(None, ("dom", "rep")),
        P(None, ("dom", "rep")),
        P(None, ("dom", "rep")),
        P(("dom", "rep")),
        P(None, "dom", None),
        P(("dom", "rep"), None, None),
        P(("dom", "rep"), None),
    )
    out_specs = (P(None, ("dom", "rep")), P(None, "dom", "rep"), P(None, None, ("dom", "rep")))
    return jax.shard_map(shards, mesh=mesh, in_specs=in_specs, out_specs=out_specs, check_vma=False)
```

```python
import functools

import jax
import jax.numpy as jnp
from jax import lax
from jax.experimental import pallas as pl
from jax.experimental.pallas import tpu as pltpu
from jax.sharding import PartitionSpec as P

GRID = 192
CELLS = GRID * GRID
LANES = 128
ROWS = CELLS // LANES
MOBILITY = 0.1
HEAD_BEADS = 8
TAIL_BEAD = 24
GROUP = 4
EARLY_BEADS = 8
VMEM_BYTES = 56 * 1024 * 1024
F32 = jnp.float32
BF16 = jnp.bfloat16


E4 = jnp.float8_e4m3fn
PIECES = 3
FORCE_SCALE = 32.0
SHARE_SCALE = 256.0


def split_e4(value):
    pieces = []
    for _ in range(PIECES):
        pieces.append(value.astype(E4))
        value = value - pieces[-1].astype(F32)
    return pieces


def split_three(value):
    high = value.astype(BF16)
    rest = value - high.astype(F32)
    mid = rest.astype(BF16)
    low = (rest - mid.astype(F32)).astype(BF16)
    return high, mid, low


def wrap_gap(gap):
    gap = jnp.where(gap >= GRID // 2, gap - GRID, gap)
    return jnp.where(gap < -(GRID // 2), gap + GRID, gap)


def ahead(plane, steps):
    rows, lanes = divmod(steps % CELLS, LANES)

    def rolled(count):
        count %= ROWS
        return jnp.concatenate([plane[count:], plane[:count]], axis=0) if count else plane

    if lanes == 0:
        return rolled(rows)
    lane = lax.broadcasted_iota(jnp.int32, plane.shape, 1)
    return pltpu.roll(jnp.where(lane >= lanes, rolled(rows), rolled(rows + 1)), LANES - lanes, 1)


def force_x(plane):
    return (ahead(plane, -GRID) - ahead(plane, GRID)) * 0.5


def force_y(plane):
    cell = lax.broadcasted_iota(jnp.int32, plane.shape, 0) * LANES
    y = lax.rem(cell + lax.broadcasted_iota(jnp.int32, plane.shape, 1), GRID)
    back = jnp.where(y == 0, ahead(plane, GRID - 1), ahead(plane, -1))
    fore = jnp.where(y == GRID - 1, ahead(plane, 1 - GRID), ahead(plane, 1))
    return (back - fore) * 0.5


def one_hot_e4(rows, key):
    return jnp.concatenate([
        jnp.where(block, jnp.ones((), E4), jnp.zeros((), E4)) for block in masks_e4(rows, key)], axis=0)


def masks_e4(rows, key):
    step = 128 if rows % 128 == 0 else 96
    lane = lax.broadcasted_iota(jnp.int8, (step, key.shape[1]), 0)
    masks = []
    for start in range(0, rows, step):
        local = key - start
        local = jnp.where((local >= 0) & (local < step), local, -1).astype(jnp.int8)
        masks.append(lane == local)
    return masks


def bead_row(ref, k, bead, chains):
    return ref[k:k + 1, pl.ds(pl.multiple_of(bead * chains, chains), chains)]


def bead_keys(cells_ref, split_ref, j, chains, layers, whole):
    cell = bead_row(cells_ref, 0, j, chains) * GRID + bead_row(cells_ref, 1, j, chains)
    column = bead_row(cells_ref, 2, j, chains) * LANES + (cell & (LANES - 1))
    if whole:
        column = column + jnp.where(j >= split_ref[...], layers * LANES, 0)
    return cell >> 7, column


def new_row(cells_ref, offsets_ref, displace_ref, k, j, push, chains, beads):
    before, after = jnp.maximum(j - 1, 0), jnp.minimum(j + 1, beads - 1)
    row = functools.partial(bead_row, chains=chains)
    cell, off = row(cells_ref, k, j), row(offsets_ref, k, j)
    gap_after = row(cells_ref, k, after) - cell
    gap_before = cell - row(cells_ref, k, before)
    if k < 2:
        gap_after, gap_before = wrap_gap(gap_after), wrap_gap(gap_before)
    gap_after = gap_after.astype(F32) + (row(offsets_ref, k, after) - off)
    gap_before = gap_before.astype(F32) + (off - row(offsets_ref, k, before))
    return off + MOBILITY * ((gap_after - gap_before) + push) + row(displace_ref, k, j)


def over_beads(body, start, stop, layers):
    half = layers * LANES
    for low, high, first, size in (
        (0, HEAD_BEADS, 0, half), (HEAD_BEADS, TAIL_BEAD, 0, 2 * half), (TAIL_BEAD, stop, half, half),
    ):
        low, high = max(low, start), min(high, stop)
        if low < high:
            pl.loop(low // GROUP, high // GROUP)(functools.partial(body, first=first, size=size))


def gather(table_ref, hot, first, parts, row):
    size, chains = hot.shape
    width = table_ref.shape[1] // PIECES
    rows = sum(
        jnp.dot(table_ref[:, p * width + first:p * width + first + size], hot, preferred_element_type=F32)
        for p in range(PIECES))
    sub = lax.broadcasted_iota(jnp.int32, (8, chains), 0)
    found = [jnp.zeros((8, chains), F32)] * parts
    for start in range(0, ROWS, 8):
        mask = sub + start == row
        for k in range(parts):
            found[k] = jnp.where(mask, rows[k * ROWS + start:k * ROWS + start + 8], found[k])
    return [jnp.sum(part, axis=0, keepdims=True) * (1 / FORCE_SCALE) for part in found]


def plane_beads(start, stop, layers, beads, chains, cells_ref, offsets_ref, displace_ref, split_ref,
                table_ref, new_ref):
    width = 2 * layers * LANES

    def body(g, first, size):
        for slot in range(GROUP):
            j = g * GROUP + slot
            row, column = bead_keys(cells_ref, split_ref, j, chains, layers, size == width)
            for k, push in enumerate(gather(table_ref, one_hot_e4(size, column), first, 2, row)):
                new_ref[k:k + 1, pl.ds(pl.multiple_of(j * chains, chains), chains)] = new_row(
                    cells_ref, offsets_ref, displace_ref, k, j, push, chains, beads)

    over_beads(body, start, stop, layers)


def early_kernel(layers, beads, chains, cells_ref, offsets_ref, displace_ref, split_ref, field_ref,
                 flat_ref, table_ref):
    width = 2 * layers * LANES
    for species in range(2):
        for layer in range(layers):
            plane = field_ref[species, layer]
            at = (species * layers + layer) * LANES
            for k, force in enumerate((force_x, force_y)):
                for p, piece in enumerate(split_e4(force(plane) * FORCE_SCALE)):
                    table_ref[k * ROWS:(k + 1) * ROWS, p * width + at:p * width + at + LANES] = piece
    plane_beads(0, EARLY_BEADS, layers, beads, chains, cells_ref, offsets_ref, displace_ref, split_ref,
                table_ref, flat_ref)


def late_kernel(layers, beads, chains, cells_ref, offsets_ref, displace_ref, split_ref, flat_ref,
                table_ref, rise_ref, chosen_ref, used_ref, new_ref, picked_ref, place_ref):
    new_ref[0:2, 0:EARLY_BEADS * chains] = flat_ref[...]
    new_ref[2:3, :] = rise_ref[...]
    plane_beads(EARLY_BEADS, beads, layers, beads, chains, cells_ref, offsets_ref, displace_ref, split_ref,
                table_ref, new_ref)

    for k in range(3):
        for j in range(beads):
            place_ref[k * beads + j:k * beads + j + 1, :] = (
                bead_row(cells_ref, k, j, chains).astype(F32) + bead_row(new_ref, k, j, chains))
    slots = chosen_ref.shape[1]
    pieces = jnp.concatenate(split_three(place_ref[...]), axis=0)
    bead_of = lax.broadcasted_iota(jnp.int32, (beads, slots), 1) // (slots // beads)
    own = bead_of == lax.broadcasted_iota(jnp.int32, (beads, slots), 0)
    slot_of = lax.broadcasted_iota(jnp.int32, (1, slots), 1) % (slots // beads)
    for way, lift in ((0, -float(layers)), (1, float(layers))):
        hot = lax.broadcasted_iota(jnp.int32, (chains, slots), 0) == chosen_ref[way:way + 1]
        hot = jnp.where(hot, 1.0, 0.0).astype(BF16)
        got = jnp.dot(pieces, hot, preferred_element_type=F32)
        kept = slot_of < used_ref[way:way + 1]
        for k in range(3):
            part = sum(got[(p * 3 + k) * beads:(p * 3 + k + 1) * beads] for p in range(3))
            line = jnp.sum(jnp.where(own, part, 0.0), axis=0, keepdims=True)
            if k == 2:
                line = line + lift
            picked_ref[way, k:k + 1, :] = jnp.where(kept, line, 0.0)


def rise_kernel(layers, beads, chains, cells_ref, offsets_ref, displace_ref, split_ref, field_ref,
                below_ref, above_ref, rise_ref, sums_ref, carry_ref,
                table_ref, hot_ref, weight_ref, total_ref):
    width = 2 * layers * LANES
    for species in range(2):
        stack = [below_ref[species]] + [field_ref[species, k] for k in range(layers)] + [above_ref[species]]
        for layer in range(layers):
            at = (species * layers + layer) * LANES
            force = (stack[layer] - stack[layer + 2]) * (0.5 * FORCE_SCALE)
            for p, piece in enumerate(split_e4(force)):
                table_ref[:, p * width + at:p * width + at + LANES] = piece
    total_ref[...] = jnp.zeros_like(total_ref)

    def body(g, first, size):
        for slot in range(GROUP):
            j = g * GROUP + slot
            lanes = slice(slot * chains, (slot + 1) * chains)
            row, column = bead_keys(cells_ref, split_ref, j, chains, layers, size == width)
            hot = one_hot_e4(size, column)
            hot_ref[0:size, lanes] = hot
            push, = gather(table_ref, hot, first, 1, row)
            new = new_row(cells_ref, offsets_ref, displace_ref, 2, j, push, chains, beads)
            rise_ref[0:1, pl.ds(pl.multiple_of(j * chains, chains), chains)] = new
            pieces = [jnp.ones(new.shape, E4)] + split_e4(jnp.clip(new, 0.0, 1.0) * SHARE_SCALE)
            for b, block in enumerate(masks_e4(ROWS, row)):
                step = block.shape[0]
                for p, piece in enumerate(pieces):
                    weight_ref[p * ROWS + b * step:p * ROWS + (b + 1) * step, lanes] = jnp.where(
                        block, jnp.broadcast_to(piece, block.shape), jnp.zeros((), E4))
        total_ref[:, first:first + size] += lax.dot_general(
            weight_ref[...], hot_ref[0:size, :], (((1,), (1,)), ((), ())), preferred_element_type=F32)

    over_beads(body, 0, beads, layers)

    shares, _, share = sums_ref.shape
    per = share // LANES

    def place(ref, slab, value):
        for r in range(shares):
            for n in range(per):
                ref[r, slab:slab + 1, n * LANES:(n + 1) * LANES] = value[r * per + n:r * per + n + 1]

    for species in range(2):
        upper = None
        for layer in range(layers):
            at = (species * layers + layer) * LANES
            count, *rises = (total_ref[p * ROWS:(p + 1) * ROWS, at:at + LANES] for p in range(1 + PIECES))
            rise = sum(rises) * (1 / SHARE_SCALE)
            place(sums_ref, layer * 2 + species, count - rise if upper is None else count - rise + upper)
            upper = rise
        place(carry_ref, species, upper)


def local_call(kernel, name, shapes, scratch, operands):
    return pl.pallas_call(
        kernel,
        out_shape=tuple(jax.ShapeDtypeStruct(shape, dtype) for shape, dtype in shapes),
        in_specs=[pl.BlockSpec(memory_space=pltpu.VMEM)] * len(operands),
        out_specs=tuple([pl.BlockSpec(memory_space=pltpu.VMEM)] * len(shapes)),
        scratch_shapes=[pltpu.VMEM(shape, dtype) for shape, dtype in scratch],
        compiler_params=pltpu.CompilerParams(vmem_limit_bytes=VMEM_BYTES),
        name=name,
    )(*operands)


def ring(value, steps):
    doms, reps = lax.axis_size("dom"), lax.axis_size("rep")
    pairs = []
    for dom in range(doms):
        for rep in range(reps):
            turn = reps // 8 if not 0 <= dom + steps < doms else 0
            pairs.append((dom * reps + rep, (dom + steps) % doms * reps + (rep ^ turn)))
    return lax.ppermute(value, ("dom", "rep"), pairs)


def shifted(value, axis, steps):
    count = lax.axis_size(axis)
    return lax.ppermute(value, axis, [(i, (i + steps) % count) for i in range(count)])


def shards(cells, offsets, displacements, block_split, fields, crossing, crossing_counts):
    chains = block_split.shape[0]
    beads = cells.shape[1] // chains
    layers = fields.shape[1]
    shares = lax.axis_size("rep")
    width = 2 * layers * LANES
    sizes = (layers, beads, chains)
    planes = fields.reshape(2, layers, ROWS, LANES)
    chosen = jnp.tile(crossing[0], (1, beads))
    used = jnp.broadcast_to(crossing_counts[0][:, None], chosen.shape)
    beads_in = (cells, offsets, displacements, block_split[None])

    below = ring(planes[:, -1], 1)
    above = ring(planes[:, 0], -1)
    flat, table = local_call(
        functools.partial(early_kernel, *sizes), "early_step",
        (((2, EARLY_BEADS * chains), F32), ((2 * ROWS, PIECES * width), E4)), (), (*beads_in, planes))
    below, above, flat = lax.optimization_barrier((below, above, flat))
    rise, sums, carry = local_call(
        functools.partial(rise_kernel, *sizes), "rise_step",
        (((1, beads * chains), F32), ((shares, 2 * layers, CELLS // shares), F32),
         ((shares, 2, CELLS // shares), F32)),
        (((ROWS, PIECES * width), E4), ((width, GROUP * chains), E4),
         (((1 + PIECES) * ROWS, GROUP * chains), E4), (((1 + PIECES) * ROWS, width), F32)),
        (*beads_in, planes, below, above))
    carried = ring(carry, 1)
    sums = sums + jnp.pad(carried, ((0, 0), (0, 2 * layers - 2), (0, 0)))
    sums, rise = lax.optimization_barrier((sums, rise))
    parts = lax.all_to_all(sums, "rep", split_axis=0, concat_axis=0, tiled=True)
    new, picked = local_call(
        functools.partial(late_kernel, *sizes), "late_step",
        (((3, beads * chains), F32), ((2, 3, chosen.shape[1]), F32)),
        (((3 * beads, chains), F32),), (*beads_in, flat, table, rise, chosen, used))
    arrived = jnp.stack([shifted(picked[0], "dom", 1), shifted(picked[1], "dom", -1)])
    density_scale = GRID * GRID * layers / (shares * chains * beads)
    density = jnp.sum(parts, axis=0) * density_scale
    return new, density.reshape(layers, 2, -1).transpose(1, 0, 2), arrived


def solution(mesh):
    in_specs = (
        P(None, ("dom", "rep")),
        P(None, ("dom", "rep")),
        P(None, ("dom", "rep")),
        P(("dom", "rep")),
        P(None, "dom", None),
        P(("dom", "rep"), None, None),
        P(("dom", "rep"), None),
    )
    out_specs = (P(None, ("dom", "rep")), P(None, "dom", "rep"), P(None, None, ("dom", "rep")))
    return jax.shard_map(shards, mesh=mesh, in_specs=in_specs, out_specs=out_specs, check_vma=False)
```

```python
import functools

import jax
import jax.numpy as jnp
from jax import lax
from jax.experimental import pallas as pl
from jax.experimental.pallas import tpu as pltpu
from jax.sharding import PartitionSpec as P

GRID = 192
CELLS = GRID * GRID
LANES = 128
ROWS = CELLS // LANES
MOBILITY = 0.1
HEAD_BEADS = 8
TAIL_BEAD = 24
GROUP = 4
FIRST_BEADS = 20
F32 = jnp.float32
BF16 = jnp.bfloat16


E4 = jnp.float8_e4m3fn
PIECES = 3
FORCE_SCALE = 32.0
SHARE_SCALE = 256.0


def split_e4(value):
    pieces = []
    for _ in range(PIECES):
        pieces.append(value.astype(E4))
        value = value - pieces[-1].astype(F32)
    return pieces


def split_three(value):
    high = value.astype(BF16)
    rest = value - high.astype(F32)
    mid = rest.astype(BF16)
    low = (rest - mid.astype(F32)).astype(BF16)
    return high, mid, low


def wrap_gap(gap):
    gap = jnp.where(gap >= GRID // 2, gap - GRID, gap)
    return jnp.where(gap < -(GRID // 2), gap + GRID, gap)


def ahead(plane, steps):
    rows, lanes = divmod(steps % CELLS, LANES)

    def rolled(count):
        count %= ROWS
        return jnp.concatenate([plane[count:], plane[:count]], axis=0) if count else plane

    if lanes == 0:
        return rolled(rows)
    lane = lax.broadcasted_iota(jnp.int32, plane.shape, 1)
    return pltpu.roll(jnp.where(lane >= lanes, rolled(rows), rolled(rows + 1)), LANES - lanes, 1)


def force_x(plane):
    return (ahead(plane, -GRID) - ahead(plane, GRID)) * 0.5


def force_y(plane):
    cell = lax.broadcasted_iota(jnp.int32, plane.shape, 0) * LANES
    y = lax.rem(cell + lax.broadcasted_iota(jnp.int32, plane.shape, 1), GRID)
    back = jnp.where(y == 0, ahead(plane, GRID - 1), ahead(plane, -1))
    fore = jnp.where(y == GRID - 1, ahead(plane, 1 - GRID), ahead(plane, 1))
    return (back - fore) * 0.5


def one_hot_e4(rows, key):
    return jnp.concatenate([
        jnp.where(block, jnp.ones((), E4), jnp.zeros((), E4)) for block in masks_e4(rows, key)], axis=0)


def masks_e4(rows, key):
    step = 128 if rows % 128 == 0 else 96
    lane = lax.broadcasted_iota(jnp.int8, (step, key.shape[1]), 0)
    masks = []
    for start in range(0, rows, step):
        local = key - start
        local = jnp.where((local >= 0) & (local < step), local, -1).astype(jnp.int8)
        masks.append(lane == local)
    return masks


def bead_row(ref, k, bead, chains):
    return ref[k:k + 1, pl.ds(pl.multiple_of(bead * chains, chains), chains)]


def key_row(x, y, z):
    cell = x * GRID + y
    return cell >> 7, z * LANES + (cell & (LANES - 1))


def bead_keys(cells_ref, split_ref, j, chains, layers, whole):
    row, column = key_row(*(bead_row(cells_ref, k, j, chains) for k in range(3)))
    if whole:
        column = column + jnp.where(j >= split_ref[...], layers * LANES, 0)
    return row, column


def base_row(cells_ref, offsets_ref, displace_ref, k, j, chains, beads):
    before, after = jnp.maximum(j - 1, 0), jnp.minimum(j + 1, beads - 1)
    row = functools.partial(bead_row, chains=chains)
    cell, off = row(cells_ref, k, j), row(offsets_ref, k, j)
    gap_after = row(cells_ref, k, after) - cell
    gap_before = cell - row(cells_ref, k, before)
    if k < 2:
        gap_after, gap_before = wrap_gap(gap_after), wrap_gap(gap_before)
    gap_after = gap_after.astype(F32) + (row(offsets_ref, k, after) - off)
    gap_before = gap_before.astype(F32) + (off - row(offsets_ref, k, before))
    return off + MOBILITY * (gap_after - gap_before) + row(displace_ref, k, j)


def over_beads(body, start, stop, layers):
    half = layers * LANES
    for low, high, first, size in (
        (0, HEAD_BEADS, 0, half), (HEAD_BEADS, TAIL_BEAD, 0, 2 * half), (TAIL_BEAD, stop, half, half),
    ):
        low, high = max(low, start), min(high, stop)
        if low < high:
            pl.loop(low // GROUP, high // GROUP)(functools.partial(body, first=first, size=size))


def gather_planes(table_ref, hot, first, row):
    size, chains = hot.shape
    width = table_ref.shape[1] // PIECES
    rows = sum(
        jnp.dot(table_ref[:, p * width + first:p * width + first + size], hot, preferred_element_type=F32)
        for p in range(PIECES))
    sub = lax.broadcasted_iota(jnp.int32, (8, chains), 0)
    found = [jnp.zeros((8, chains), F32)] * 2
    for block in range(ROWS // 8):
        mask = sub + 8 * block == row
        for k in range(2):
            at = 8 * (block * 2 + k)
            found[k] = jnp.where(mask, rows[at:at + 8], found[k])
    return [jnp.sum(part, axis=0, keepdims=True) * (1 / FORCE_SCALE) for part in found]


def write_planes(table_ref, at, forces):
    width = table_ref.shape[1] // PIECES
    rows = jnp.concatenate(
        [force[8 * block:8 * block + 8] for block in range(ROWS // 8) for force in forces], axis=0)
    for p, piece in enumerate(split_e4(rows * FORCE_SCALE)):
        table_ref[:, p * width + at:p * width + at + LANES] = piece


def gather_rise(table_ref, hot, first, row):
    size, chains = hot.shape
    rows = jnp.dot(table_ref[:, first:first + size], hot, preferred_element_type=F32)
    sub = lax.broadcasted_iota(jnp.int32, (8, chains), 0)
    found = [jnp.zeros((8, chains), F32)] * PIECES
    for block in range(ROWS // 8):
        mask = sub + 8 * block == row
        for p in range(PIECES):
            at = 8 * (block * PIECES + p)
            found[p] = jnp.where(mask, rows[at:at + 8], found[p])
    return jnp.sum(sum(found), axis=0, keepdims=True) * (1 / FORCE_SCALE)


def write_rise(table_ref, at, force):
    pieces = [piece.astype(F32) for piece in split_e4(force * FORCE_SCALE)]
    rows = [piece[8 * block:8 * block + 8] for block in range(ROWS // 8) for piece in pieces]
    table_ref[:, at:at + LANES] = jnp.concatenate(rows, axis=0).astype(E4)


def plane_beads(start, stop, layers, chains, cells_ref, split_ref, base_ref, table_ref, new_ref):
    width = 2 * layers * LANES

    def body(g, first, size):
        for slot in range(GROUP):
            j = g * GROUP + slot
            row, column = bead_keys(cells_ref, split_ref, j, chains, layers, size == width)
            for k, push in enumerate(gather_planes(table_ref, one_hot_e4(size, column), first, row)):
                new_ref[k:k + 1, pl.ds(pl.multiple_of(j * chains, chains), chains)] = (
                    bead_row(base_ref, k, j, chains) + MOBILITY * push)

    over_beads(body, start, stop, layers)


def slot_lanes(beads, slots):
    lane = lax.broadcasted_iota(jnp.int32, (1, beads * slots), 1)
    return lane // slots, lane % slots


def picker(chosen_ref, way, beads, chains):
    slots = chosen_ref.shape[2]
    chosen = jnp.concatenate([chosen_ref[0, way:way + 1, :]] * beads, axis=1)
    hot = lax.broadcasted_iota(jnp.int32, (chains, beads * slots), 0) == chosen
    hot = jnp.where(hot, 1.0, 0.0).astype(BF16)
    bead_of, _ = slot_lanes(beads, slots)
    own = lax.broadcasted_iota(jnp.int32, (beads, beads * slots), 0) == bead_of

    def pick(pieces):
        got = jnp.dot(jnp.concatenate(pieces, axis=0), hot, preferred_element_type=F32)
        return [
            jnp.sum(jnp.where(own, got[p * beads:(p + 1) * beads], 0.0), axis=0, keepdims=True)
            for p in range(len(pieces))
        ]

    return pick


def early_kernel(layers, beads, chains, cells_ref, offsets_ref, displace_ref, split_ref, field_ref,
                 chosen_ref, used_ref, base_ref, table_ref, picked_ref, place_ref):
    width = 2 * layers * LANES
    for species in range(2):
        for layer in range(layers):
            plane = field_ref[species, layer]
            at = (species * layers + layer) * LANES
            write_planes(table_ref, at, [force_x(plane), force_y(plane)])

    @pl.loop(0, beads)
    def _(j):
        for k in range(3):
            place_ref[k, pl.ds(j, 1), :] = bead_row(cells_ref, k, j, chains).astype(F32)
        for k in range(2):
            row = base_row(cells_ref, offsets_ref, displace_ref, k, j, chains, beads)
            base_ref[k:k + 1, pl.ds(pl.multiple_of(j * chains, chains), chains)] = row
            place_ref[3 + k, pl.ds(j, 1), :] = row

    cells = [place_ref[k].astype(BF16) for k in range(3)]
    bases = [piece for k in range(2) for piece in split_three(place_ref[3 + k])]
    split = jnp.broadcast_to(split_ref[...], (beads, chains)).astype(F32).astype(BF16)
    bead_of, slot_of = slot_lanes(beads, chosen_ref.shape[2])
    for way in range(2):
        x, y, z, edge, *pieces = picker(chosen_ref, way, beads, chains)([*cells, split, *bases])
        row, column = key_row(*(value.astype(jnp.int32) for value in (x, y, z)))
        column = column + jnp.where(bead_of >= edge.astype(jnp.int32), layers * LANES, 0)
        pushes = gather_planes(table_ref, one_hot_e4(width, column), 0, row)
        kept = slot_of < used_ref[0, way]
        for k, (cell, push) in enumerate(zip((x, y), pushes)):
            base = sum(pieces[3 * k:3 * k + 3])
            picked_ref[way, k:k + 1, :] = jnp.where(kept, cell + (base + MOBILITY * push), 0.0)


def first_kernel(start, stop, layers, chains, *refs):
    plane_beads(start, stop, layers, chains, *refs)


def rest_kernel(start, stop, layers, chains, cells_ref, split_ref, base_ref, table_ref, flat_ref, rise_ref, new_ref):
    new_ref[0:2, 0:start * chains] = flat_ref[...]
    new_ref[2:3, :] = rise_ref[...]
    plane_beads(start, stop, layers, chains, cells_ref, split_ref, base_ref, table_ref, new_ref)


def rise_kernel(layers, beads, chains, cells_ref, offsets_ref, displace_ref, split_ref, field_ref,
                below_ref, above_ref, chosen_ref, used_ref, picked_ref, rise_ref, sums_ref, carry_ref, fall_ref,
                table_ref, hot_ref, weight_ref, total_ref, place_ref):
    width = 2 * layers * LANES
    for species in range(2):
        stack = [below_ref[species]] + [field_ref[species, k] for k in range(layers)] + [above_ref[species]]
        for layer in range(layers):
            at = (species * layers + layer) * LANES
            write_rise(table_ref, at, (stack[layer] - stack[layer + 2]) * 0.5)
    total_ref[...] = jnp.zeros_like(total_ref)

    def body(g, first, size):
        for slot in range(GROUP):
            j = g * GROUP + slot
            lanes = slice(slot * chains, (slot + 1) * chains)
            row, column = bead_keys(cells_ref, split_ref, j, chains, layers, size == width)
            hot = one_hot_e4(size, column)
            hot_ref[0:size, lanes] = hot
            push = gather_rise(table_ref, hot, first, row)
            new = base_row(cells_ref, offsets_ref, displace_ref, 2, j, chains, beads) + MOBILITY * push
            place_ref[pl.ds(j, 1), :] = bead_row(cells_ref, 2, j, chains).astype(F32) + new
            rise_ref[0:1, pl.ds(pl.multiple_of(j * chains, chains), chains)] = new
            pieces = [jnp.ones(new.shape, E4)] + split_e4(jnp.clip(new, 0.0, 1.0) * SHARE_SCALE)
            for b, block in enumerate(masks_e4(ROWS, row)):
                step = block.shape[0]
                for p, piece in enumerate(pieces):
                    weight_ref[p * ROWS + b * step:p * ROWS + (b + 1) * step, lanes] = jnp.where(
                        block, jnp.broadcast_to(piece, block.shape), jnp.zeros((), E4))
        total_ref[:, first:first + size] += lax.dot_general(
            weight_ref[...], hot_ref[0:size, :], (((1,), (1,)), ((), ())), preferred_element_type=F32)

    over_beads(body, 0, beads, layers)

    blocks = sums_ref.shape[0]
    per = ROWS // (2 * blocks)
    places = [rep_place(2 * blocks, rep) for rep in range(2 * blocks)]
    for species in range(2):
        upper = None
        for layer in range(layers):
            at = (species * layers + layer) * LANES
            count, *rises = (total_ref[p * ROWS:(p + 1) * ROWS, at:at + LANES] for p in range(1 + PIECES))
            rise = sum(rises) * (1 / SHARE_SCALE)
            lower = count - rise if upper is None else count - rise + upper
            for rep, (block, half) in enumerate(places):
                slab = (half * 2 * layers + layer * 2 + species) * per
                sums_ref[block, slab:slab + per, :] = lower[rep * per:(rep + 1) * per]
            upper = rise
        for rep, (block, half) in enumerate(places):
            slab = (half * 2 + species) * per
            carry_ref[block, slab:slab + per, :] = upper[rep * per:(rep + 1) * per]

    def lay(ref, line):
        for k in range(3):
            for n in range(chains // LANES):
                at = k * (chains // LANES) + n
                ref[at:at + 1, :] = line[k][:, n * LANES:(n + 1) * LANES]

    slots = chosen_ref.shape[2]
    carry_ref[blocks] = jnp.zeros(carry_ref.shape[1:], F32)
    pieces = split_three(place_ref[...])
    _, slot_of = slot_lanes(beads, slots)
    for way, (ref, lift) in enumerate(((carry_ref.at[blocks], -float(layers)), (fall_ref, float(layers)))):
        line = sum(picker(chosen_ref, way, beads, chains)(pieces)) + lift
        line = jnp.where(slot_of < used_ref[0, way], line, 0.0)
        lay(ref, [picked_ref[way, 0:1, :], picked_ref[way, 1:2, :], line])


def merge_kernel(sums_ref, carried_ref, merged_ref):
    blocks, rows, _ = sums_ref.shape
    merged_ref[...] = sums_ref[...]
    for half in range(2):
        at, carry = slice(half * rows // 2, half * rows // 2 + rows // 4), slice(half * rows // 4, (half + 1) * rows // 4)
        merged_ref[:, at, :] = sums_ref[:, at, :] + carried_ref[0:blocks, carry, :]


def fold_kernel(parts_ref, carried_ref, fallen_ref, folded_ref):
    blocks, rows, _ = parts_ref.shape
    extra = fallen_ref.shape[0]
    total = jnp.sum(parts_ref[...], axis=0)
    for half in range(2):
        folded_ref[half, 0:rows // 2, :] = total[half * rows // 2:(half + 1) * rows // 2]
        folded_ref[half, rows // 2:rows // 2 + extra, :] = carried_ref[blocks, 0:extra, :]
        folded_ref[half, rows // 2 + extra:, :] = fallen_ref[...]


def last_kernel(layers, scale, both_ref, carried_ref, fallen_ref, own_ref, density_ref, arrived_ref):
    blocks = carried_ref.shape[0] - 1
    per = density_ref.shape[2] // LANES
    rows, extra = 2 * layers * per, fallen_ref.shape[0]
    total = (both_ref[0, 0:rows, :] + both_ref[1, 0:rows, :]) * scale
    for layer in range(layers):
        for species in range(2):
            for n in range(per):
                at = (layer * 2 + species) * per + n
                density_ref[species, layer:layer + 1, n * LANES:(n + 1) * LANES] = total[at:at + 1]
    other = jnp.where(own_ref[0] == 0, both_ref[1, rows:, :], both_ref[0, rows:, :])
    up = jnp.where(own_ref[1] == 1, other[0:extra], carried_ref[blocks, 0:extra, :])
    down = jnp.where(own_ref[2] == 1, other[extra:], fallen_ref[...])
    for way, came in enumerate((up, down)):
        for k in range(3):
            for n in range(extra // 3):
                at = k * (extra // 3) + n
                arrived_ref[k, way:way + 1, n * LANES:(n + 1) * LANES] = came[at:at + 1]


def local_call(kernel, name, shapes, scratch, operands, scalars=(), limit=24):
    return pl.pallas_call(
        kernel,
        out_shape=tuple(jax.ShapeDtypeStruct(shape, dtype) for shape, dtype in shapes),
        in_specs=[
            pl.BlockSpec(memory_space=pltpu.SMEM if n in scalars else pltpu.VMEM) for n in range(len(operands))],
        out_specs=tuple([pl.BlockSpec(memory_space=pltpu.VMEM)] * len(shapes)),
        scratch_shapes=[pltpu.VMEM(shape, dtype) for shape, dtype in scratch],
        compiler_params=pltpu.CompilerParams(vmem_limit_bytes=limit * 1024 * 1024),
        name=name,
    )(*operands)


def rep_place(reps, rep):
    turn = reps // 8
    return rep // (2 * turn) * turn + rep % turn, rep // turn % 2


def rep_groups(reps):
    halves = [[rep for rep in range(reps) if rep_place(reps, rep)[1] == half] for half in range(2)]
    return halves, [list(pair) for pair in zip(*halves)]


def exchange(value, groups):
    return lax.all_to_all(value, "rep", split_axis=0, concat_axis=0, tiled=True, axis_index_groups=groups)


def ring(value, steps):
    doms, reps = lax.axis_size("dom"), lax.axis_size("rep")
    pairs = []
    for dom in range(doms):
        for rep in range(reps):
            turn = 0 if 0 <= dom + steps < doms else reps // 8
            pairs.append((dom * reps + rep, (dom + steps) % doms * reps + (rep ^ turn)))
    return lax.ppermute(value, ("dom", "rep"), pairs)


def shards(cells, offsets, displacements, block_split, fields, crossing, crossing_counts):
    chains = block_split.shape[0]
    beads = cells.shape[1] // chains
    layers = fields.shape[1]
    doms, reps = lax.axis_size("dom"), lax.axis_size("rep")
    dom, rep = lax.axis_index("dom"), lax.axis_index("rep")
    blocks, extra = reps // 2, 3 * chains // LANES
    rows = 4 * layers * (ROWS // reps)
    halves, pairs = rep_groups(reps)
    width = 2 * layers * LANES
    sizes = (layers, beads, chains)
    planes = fields.reshape(2, layers, ROWS, LANES)
    split = block_split[None]
    beads_in = (cells, offsets, displacements, split)
    own = jnp.stack([rep_place(reps, rep)[1], dom == 0, dom == doms - 1]).astype(jnp.int32)

    below = ring(planes[:, -1], 1)
    above = ring(planes[:, 0], -1)
    base, table, picked = local_call(
        functools.partial(early_kernel, *sizes), "early_step",
        (((2, beads * chains), F32), ((2 * ROWS, PIECES * width), E4), ((2, 2, chains), F32)),
        (((5, beads, chains), F32),), (*beads_in, planes, crossing, crossing_counts), (6,))
    below, above, picked = lax.optimization_barrier((below, above, picked))
    rise, sums, carry, fall = local_call(
        functools.partial(rise_kernel, *sizes), "rise_step",
        (((1, beads * chains), F32), ((blocks, rows, LANES), F32),
         ((blocks + 1, rows // 2, LANES), F32), ((extra, LANES), F32)),
        (((PIECES * ROWS, width), E4), ((width, GROUP * chains), E4),
         (((1 + PIECES) * ROWS, GROUP * chains), E4), (((1 + PIECES) * ROWS, width), F32), ((beads, chains), F32)),
        (*beads_in, planes, below, above, crossing, crossing_counts, picked), (8,))
    carried, fallen = ring(carry, 1), ring(fall, -1)
    merged, = local_call(
        merge_kernel, "merge_step", (((blocks, rows, LANES), F32),), (), (sums, carried), limit=8)

    merged, base = lax.optimization_barrier((merged, base))
    parts = exchange(merged, halves)
    flat, = local_call(
        functools.partial(first_kernel, 0, FIRST_BEADS, layers, chains), "first_step",
        (((2, FIRST_BEADS * chains), F32),), (), (cells, split, base, table))
    parts, flat = lax.optimization_barrier((parts, flat))
    folded, = local_call(
        fold_kernel, "fold_step", (((2, rows // 2 + 2 * extra, LANES), F32),), (), (parts, carried, fallen), limit=8)
    folded, base = lax.optimization_barrier((folded, base))
    both = exchange(folded, pairs)
    new, = local_call(
        functools.partial(rest_kernel, FIRST_BEADS, beads, layers, chains), "rest_step",
        (((3, beads * chains), F32),), (), (cells, split, base, table, flat, rise))
    both, new = lax.optimization_barrier((both, new))
    density_scale = GRID * GRID * layers / (reps * chains * beads)
    density, arrived = local_call(
        functools.partial(last_kernel, layers, density_scale), "last_step",
        (((2, layers, CELLS // reps), F32), ((3, 2, chains), F32)), (), (both, carried, fallen, own), (3,), limit=8)
    return new, density, arrived.transpose(1, 0, 2)


def solution(mesh):
    in_specs = (
        P(None, ("dom", "rep")),
        P(None, ("dom", "rep")),
        P(None, ("dom", "rep")),
        P(("dom", "rep")),
        P(None, "dom", None),
        P(("dom", "rep"), None, None),
        P(("dom", "rep"), None),
    )
    out_specs = (P(None, ("dom", "rep")), P(None, "dom", "rep"), P(None, None, ("dom", "rep")))
    return jax.shard_map(shards, mesh=mesh, in_specs=in_specs, out_specs=out_specs, check_vma=False)
```

```python
import functools

import jax
import jax.numpy as jnp
from jax import lax
from jax.experimental import pallas as pl
from jax.experimental.pallas import tpu as pltpu
from jax.sharding import PartitionSpec as P

GRID = 192
CELLS = GRID * GRID
LANES = 128
ROWS = CELLS // LANES
MOBILITY = 0.1
HEAD_BEADS = 8
TAIL_BEAD = 24
GROUP = 8
HALF_GROUP = 4
FIRST_BEADS = 16
F32 = jnp.float32
BF16 = jnp.bfloat16


E4 = jnp.float8_e4m3fn
PIECES = 3
FORCE_SCALE = 32.0
SHARE_SCALE = 256.0


def split_e4(value):
    pieces = []
    for _ in range(PIECES):
        pieces.append(value.astype(E4))
        value = value - pieces[-1].astype(F32)
    return pieces


def split_three(value):
    high = value.astype(BF16)
    rest = value - high.astype(F32)
    mid = rest.astype(BF16)
    low = (rest - mid.astype(F32)).astype(BF16)
    return high, mid, low


def wrap_gap(gap):
    gap = jnp.where(gap >= GRID // 2, gap - GRID, gap)
    return jnp.where(gap < -(GRID // 2), gap + GRID, gap)


def ahead(plane, steps):
    rows, lanes = divmod(steps % CELLS, LANES)

    def rolled(count):
        count %= ROWS
        return jnp.concatenate([plane[count:], plane[:count]], axis=0) if count else plane

    if lanes == 0:
        return rolled(rows)
    lane = lax.broadcasted_iota(jnp.int32, plane.shape, 1)
    return pltpu.roll(jnp.where(lane >= lanes, rolled(rows), rolled(rows + 1)), LANES - lanes, 1)


def force_x(plane):
    return (ahead(plane, -GRID) - ahead(plane, GRID)) * 0.5


def force_y(plane):
    cell = lax.broadcasted_iota(jnp.int32, plane.shape, 0) * LANES
    y = lax.rem(cell + lax.broadcasted_iota(jnp.int32, plane.shape, 1), GRID)
    back = jnp.where(y == 0, ahead(plane, GRID - 1), ahead(plane, -1))
    fore = jnp.where(y == GRID - 1, ahead(plane, 1 - GRID), ahead(plane, 1))
    return (back - fore) * 0.5


def one_hot_e4(rows, key):
    return jnp.concatenate([
        jnp.where(block, jnp.ones((), E4), jnp.zeros((), E4)) for block in masks_e4(rows, key)], axis=0)


def masks_e4(rows, key):
    step = 128 if rows % 128 == 0 else 96
    lane = lax.broadcasted_iota(jnp.int8, (step, key.shape[1]), 0)
    masks = []
    for start in range(0, rows, step):
        local = key - start
        local = jnp.where((local >= 0) & (local < step), local, -1).astype(jnp.int8)
        masks.append(lane == local)
    return masks


def bead_row(ref, k, bead, chains):
    return ref[k:k + 1, pl.ds(pl.multiple_of(bead * chains, chains), chains)]


def key_row(x, y, z):
    cell = x * GRID + y
    return cell >> 7, z * LANES + (cell & (LANES - 1))


def bead_keys(cells_ref, split_ref, j, chains, layers, whole):
    row, column = key_row(*(bead_row(cells_ref, k, j, chains) for k in range(3)))
    if whole:
        column = column + jnp.where(j >= split_ref[...], layers * LANES, 0)
    return row, column


def base_row(cells_ref, offsets_ref, displace_ref, k, j, chains, beads):
    before, after = jnp.maximum(j - 1, 0), jnp.minimum(j + 1, beads - 1)
    row = functools.partial(bead_row, chains=chains)
    cell, off = row(cells_ref, k, j), row(offsets_ref, k, j)
    gap_after = row(cells_ref, k, after) - cell
    gap_before = cell - row(cells_ref, k, before)
    if k < 2:
        gap_after, gap_before = wrap_gap(gap_after), wrap_gap(gap_before)
    gap_after = gap_after.astype(F32) + (row(offsets_ref, k, after) - off)
    gap_before = gap_before.astype(F32) + (off - row(offsets_ref, k, before))
    return off + MOBILITY * (gap_after - gap_before) + row(displace_ref, k, j)


def over_beads(body, start, stop, layers):
    half = layers * LANES
    for low, high, first, size in (
        (0, HEAD_BEADS, 0, half), (HEAD_BEADS, TAIL_BEAD, 0, 2 * half), (TAIL_BEAD, stop, half, half),
    ):
        low, high = max(low, start), min(high, stop)
        if low < high:
            pl.loop(low // GROUP, high // GROUP)(functools.partial(body, first=first, size=size))


def gather_planes(table_ref, hot, first, row):
    size, chains = hot.shape
    width = table_ref.shape[1] // PIECES
    rows = sum(
        jnp.dot(table_ref[:, p * width + first:p * width + first + size], hot, preferred_element_type=F32)
        for p in range(PIECES))
    sub = lax.broadcasted_iota(jnp.int32, (8, chains), 0)
    found = [jnp.zeros((8, chains), F32)] * 2
    for block in range(ROWS // 8):
        mask = sub + 8 * block == row
        for k in range(2):
            at = 8 * (block * 2 + k)
            found[k] = jnp.where(mask, rows[at:at + 8], found[k])
    return [jnp.sum(part, axis=0, keepdims=True) * (1 / FORCE_SCALE) for part in found]


def write_planes(table_ref, at, forces):
    width = table_ref.shape[1] // PIECES
    rows = jnp.concatenate(
        [force[8 * block:8 * block + 8] for block in range(ROWS // 8) for force in forces], axis=0)
    for p, piece in enumerate(split_e4(rows * FORCE_SCALE)):
        table_ref[:, p * width + at:p * width + at + LANES] = piece


def gather_rise(table_ref, hot, first, row):
    size, chains = hot.shape
    rows = jnp.dot(table_ref[:, first:first + size], hot, preferred_element_type=F32)
    sub = lax.broadcasted_iota(jnp.int32, (8, chains), 0)
    found = [jnp.zeros((8, chains), F32)] * PIECES
    for block in range(ROWS // 8):
        mask = sub + 8 * block == row
        for p in range(PIECES):
            at = 8 * (block * PIECES + p)
            found[p] = jnp.where(mask, rows[at:at + 8], found[p])
    return jnp.sum(sum(found), axis=0, keepdims=True) * (1 / FORCE_SCALE)


def write_rise(table_ref, at, force):
    pieces = [piece.astype(F32) for piece in split_e4(force * FORCE_SCALE)]
    rows = [piece[8 * block:8 * block + 8] for block in range(ROWS // 8) for piece in pieces]
    table_ref[:, at:at + LANES] = jnp.concatenate(rows, axis=0).astype(E4)


def plane_beads(start, stop, layers, chains, cells_ref, split_ref, base_ref, table_ref, new_ref):
    width = 2 * layers * LANES

    def body(g, first, size):
        for slot in range(GROUP):
            j = g * GROUP + slot
            row, column = bead_keys(cells_ref, split_ref, j, chains, layers, size == width)
            for k, push in enumerate(gather_planes(table_ref, one_hot_e4(size, column), first, row)):
                new_ref[k:k + 1, pl.ds(pl.multiple_of(j * chains, chains), chains)] = (
                    bead_row(base_ref, k, j, chains) + MOBILITY * push)

    over_beads(body, start, stop, layers)


def slot_lanes(beads, slots):
    lane = lax.broadcasted_iota(jnp.int32, (1, beads * slots), 1)
    return lane // slots, lane % slots


def picker(chosen_ref, way, beads, chains):
    slots = chosen_ref.shape[2]
    chosen = jnp.concatenate([chosen_ref[0, way:way + 1, :]] * beads, axis=1)
    hot = lax.broadcasted_iota(jnp.int32, (chains, beads * slots), 0) == chosen
    hot = jnp.where(hot, 1.0, 0.0).astype(BF16)
    bead_of, _ = slot_lanes(beads, slots)
    own = lax.broadcasted_iota(jnp.int32, (beads, beads * slots), 0) == bead_of

    def pick(pieces):
        got = jnp.dot(jnp.concatenate(pieces, axis=0), hot, preferred_element_type=F32)
        return [
            jnp.sum(jnp.where(own, got[p * beads:(p + 1) * beads], 0.0), axis=0, keepdims=True)
            for p in range(len(pieces))
        ]

    return pick


def early_kernel(layers, beads, chains, cells_ref, offsets_ref, displace_ref, split_ref, field_ref,
                 chosen_ref, used_ref, base_ref, table_ref, picked_ref, place_ref):
    width = 2 * layers * LANES
    for species in range(2):
        for layer in range(layers):
            plane = field_ref[species, layer]
            at = (species * layers + layer) * LANES
            write_planes(table_ref, at, [force_x(plane), force_y(plane)])

    @pl.loop(0, beads)
    def _(j):
        for k in range(3):
            place_ref[k, pl.ds(j, 1), :] = bead_row(cells_ref, k, j, chains).astype(F32)
        for k in range(2):
            row = base_row(cells_ref, offsets_ref, displace_ref, k, j, chains, beads)
            base_ref[k:k + 1, pl.ds(pl.multiple_of(j * chains, chains), chains)] = row
            place_ref[3 + k, pl.ds(j, 1), :] = row

    cells = [place_ref[k].astype(BF16) for k in range(3)]
    bases = [piece for k in range(2) for piece in split_three(place_ref[3 + k])]
    split = jnp.broadcast_to(split_ref[...], (beads, chains)).astype(F32).astype(BF16)
    bead_of, slot_of = slot_lanes(beads, chosen_ref.shape[2])
    for way in range(2):
        x, y, z, edge, *pieces = picker(chosen_ref, way, beads, chains)([*cells, split, *bases])
        row, column = key_row(*(value.astype(jnp.int32) for value in (x, y, z)))
        column = column + jnp.where(bead_of >= edge.astype(jnp.int32), layers * LANES, 0)
        pushes = gather_planes(table_ref, one_hot_e4(width, column), 0, row)
        kept = slot_of < used_ref[0, way]
        for k, (cell, push) in enumerate(zip((x, y), pushes)):
            base = sum(pieces[3 * k:3 * k + 3])
            picked_ref[way, k:k + 1, :] = jnp.where(kept, cell + (base + MOBILITY * push), 0.0)


def first_kernel(start, stop, layers, chains, *refs):
    plane_beads(start, stop, layers, chains, *refs)


def rest_kernel(start, stop, layers, chains, cells_ref, split_ref, base_ref, table_ref, flat_ref, rise_ref, new_ref):
    new_ref[0:2, 0:start * chains] = flat_ref[...]
    new_ref[2:3, :] = rise_ref[...]
    plane_beads(start, stop, layers, chains, cells_ref, split_ref, base_ref, table_ref, new_ref)


def rise_kernel(layers, beads, chains, cells_ref, offsets_ref, displace_ref, split_ref, field_ref,
                below_ref, above_ref, chosen_ref, used_ref, picked_ref, rise_ref, sums_ref, carry_ref, fall_ref,
                table_ref, hot_refs, weight_refs, total_ref, place_ref):
    width = 2 * layers * LANES
    for species in range(2):
        stack = [below_ref[species]] + [field_ref[species, k] for k in range(layers)] + [above_ref[species]]
        for layer in range(layers):
            at = (species * layers + layer) * LANES
            write_rise(table_ref, at, (stack[layer] - stack[layer + 2]) * 0.5)
    total_ref[...] = jnp.zeros_like(total_ref)

    def move(j, slot, first, size, hot_ref, weight_ref):
        lanes = slice(slot * chains, (slot + 1) * chains)
        row, column = bead_keys(cells_ref, split_ref, j, chains, layers, size == width)
        hot = one_hot_e4(size, column)
        hot_ref[0:size, lanes] = hot
        push = gather_rise(table_ref, hot, first, row)
        new = base_row(cells_ref, offsets_ref, displace_ref, 2, j, chains, beads) + MOBILITY * push
        place_ref[pl.ds(j, 1), :] = bead_row(cells_ref, 2, j, chains).astype(F32) + new
        rise_ref[0:1, pl.ds(pl.multiple_of(j * chains, chains), chains)] = new
        pieces = [jnp.ones(new.shape, E4)] + split_e4(jnp.clip(new, 0.0, 1.0) * SHARE_SCALE)
        for b, block in enumerate(masks_e4(ROWS, row)):
            step = block.shape[0]
            for p, piece in enumerate(pieces):
                weight_ref[p * ROWS + b * step:p * ROWS + (b + 1) * step, lanes] = jnp.where(
                    block, jnp.broadcast_to(piece, block.shape), jnp.zeros((), E4))

    def body(g, first, size):
        def add_up(half, low, high):
            total_ref[low:high, first:first + size] += lax.dot_general(
                weight_refs[half][low:high, :], hot_refs[half][0:size, :], (((1,), (1,)), ((), ())),
                preferred_element_type=F32)

        for slot in range(HALF_GROUP):
            move(g * GROUP + slot, slot, first, size, hot_refs[0], weight_refs[0])
        for slot in range(HALF_GROUP):
            move(g * GROUP + HALF_GROUP + slot, slot, first, size, hot_refs[1], weight_refs[1])
            add_up(0, slot * ROWS, (slot + 1) * ROWS)
        add_up(1, 0, weight_refs[1].shape[0])

    over_beads(body, 0, beads, layers)

    blocks = sums_ref.shape[0]
    per = ROWS // (2 * blocks)
    places = [rep_place(2 * blocks, rep) for rep in range(2 * blocks)]
    for species in range(2):
        upper = None
        for layer in range(layers):
            at = (species * layers + layer) * LANES
            count, *rises = (total_ref[p * ROWS:(p + 1) * ROWS, at:at + LANES] for p in range(1 + PIECES))
            rise = sum(rises) * (1 / SHARE_SCALE)
            lower = count - rise if upper is None else count - rise + upper
            for rep, (block, half) in enumerate(places):
                slab = (half * 2 * layers + layer * 2 + species) * per
                sums_ref[block, slab:slab + per, :] = lower[rep * per:(rep + 1) * per]
            upper = rise
        for rep, (block, half) in enumerate(places):
            slab = (half * 2 + species) * per
            carry_ref[block, slab:slab + per, :] = upper[rep * per:(rep + 1) * per]

    def lay(ref, line):
        for k in range(3):
            for n in range(chains // LANES):
                at = k * (chains // LANES) + n
                ref[at:at + 1, :] = line[k][:, n * LANES:(n + 1) * LANES]

    slots = chosen_ref.shape[2]
    carry_ref[blocks] = jnp.zeros(carry_ref.shape[1:], F32)
    pieces = split_three(place_ref[...])
    _, slot_of = slot_lanes(beads, slots)
    for way, (ref, lift) in enumerate(((carry_ref.at[blocks], -float(layers)), (fall_ref, float(layers)))):
        line = sum(picker(chosen_ref, way, beads, chains)(pieces)) + lift
        line = jnp.where(slot_of < used_ref[0, way], line, 0.0)
        lay(ref, [picked_ref[way, 0:1, :], picked_ref[way, 1:2, :], line])


def merge_kernel(sums_ref, carried_ref, merged_ref):
    blocks, rows, _ = sums_ref.shape
    merged_ref[...] = sums_ref[...]
    for half in range(2):
        at, carry = slice(half * rows // 2, half * rows // 2 + rows // 4), slice(half * rows // 4, (half + 1) * rows // 4)
        merged_ref[:, at, :] = sums_ref[:, at, :] + carried_ref[0:blocks, carry, :]


def fold_kernel(parts_ref, carried_ref, fallen_ref, folded_ref):
    blocks, rows, _ = parts_ref.shape
    extra = fallen_ref.shape[0]
    total = jnp.sum(parts_ref[...], axis=0)
    for half in range(2):
        folded_ref[half, 0:rows // 2, :] = total[half * rows // 2:(half + 1) * rows // 2]
        folded_ref[half, rows // 2:rows // 2 + extra, :] = carried_ref[blocks, 0:extra, :]
        folded_ref[half, rows // 2 + extra:, :] = fallen_ref[...]


def last_kernel(layers, scale, both_ref, carried_ref, fallen_ref, own_ref, density_ref, arrived_ref):
    blocks = carried_ref.shape[0] - 1
    per = density_ref.shape[2] // LANES
    rows, extra = 2 * layers * per, fallen_ref.shape[0]
    total = (both_ref[0, 0:rows, :] + both_ref[1, 0:rows, :]) * scale
    for layer in range(layers):
        for species in range(2):
            for n in range(per):
                at = (layer * 2 + species) * per + n
                density_ref[species, layer:layer + 1, n * LANES:(n + 1) * LANES] = total[at:at + 1]
    other = jnp.where(own_ref[0] == 0, both_ref[1, rows:, :], both_ref[0, rows:, :])
    up = jnp.where(own_ref[1] == 1, other[0:extra], carried_ref[blocks, 0:extra, :])
    down = jnp.where(own_ref[2] == 1, other[extra:], fallen_ref[...])
    for way, came in enumerate((up, down)):
        for k in range(3):
            for n in range(extra // 3):
                at = k * (extra // 3) + n
                arrived_ref[k, way:way + 1, n * LANES:(n + 1) * LANES] = came[at:at + 1]


def local_call(kernel, name, shapes, scratch, operands, scalars=(), limit=24):
    return pl.pallas_call(
        kernel,
        out_shape=tuple(jax.ShapeDtypeStruct(shape, dtype) for shape, dtype in shapes),
        in_specs=[
            pl.BlockSpec(memory_space=pltpu.SMEM if n in scalars else pltpu.VMEM) for n in range(len(operands))],
        out_specs=tuple([pl.BlockSpec(memory_space=pltpu.VMEM)] * len(shapes)),
        scratch_shapes=[
            [pltpu.VMEM(*one) for one in entry] if isinstance(entry, list) else pltpu.VMEM(*entry)
            for entry in scratch],
        compiler_params=pltpu.CompilerParams(vmem_limit_bytes=limit * 1024 * 1024),
        name=name,
    )(*operands)


def rep_place(reps, rep):
    turn = reps // 8
    return rep // (2 * turn) * turn + rep % turn, rep // turn % 2


def rep_groups(reps):
    halves = [[rep for rep in range(reps) if rep_place(reps, rep)[1] == half] for half in range(2)]
    return halves, [list(pair) for pair in zip(*halves)]


def exchange(value, groups):
    return lax.all_to_all(value, "rep", split_axis=0, concat_axis=0, tiled=True, axis_index_groups=groups)


def ring(value, steps):
    doms, reps = lax.axis_size("dom"), lax.axis_size("rep")
    pairs = []
    for dom in range(doms):
        for rep in range(reps):
            turn = 0 if 0 <= dom + steps < doms else reps // 8
            pairs.append((dom * reps + rep, (dom + steps) % doms * reps + (rep ^ turn)))
    return lax.ppermute(value, ("dom", "rep"), pairs)


def shards(cells, offsets, displacements, block_split, fields, crossing, crossing_counts):
    chains = block_split.shape[0]
    beads = cells.shape[1] // chains
    layers = fields.shape[1]
    doms, reps = lax.axis_size("dom"), lax.axis_size("rep")
    dom, rep = lax.axis_index("dom"), lax.axis_index("rep")
    blocks, extra = reps // 2, 3 * chains // LANES
    rows = 4 * layers * (ROWS // reps)
    halves, pairs = rep_groups(reps)
    width = 2 * layers * LANES
    sizes = (layers, beads, chains)
    planes = fields.reshape(2, layers, ROWS, LANES)
    split = block_split[None]
    beads_in = (cells, offsets, displacements, split)
    own = jnp.stack([rep_place(reps, rep)[1], dom == 0, dom == doms - 1]).astype(jnp.int32)

    below = ring(planes[:, -1], 1)
    above = ring(planes[:, 0], -1)
    base, table, picked = local_call(
        functools.partial(early_kernel, *sizes), "early_step",
        (((2, beads * chains), F32), ((2 * ROWS, PIECES * width), E4), ((2, 2, chains), F32)),
        (((5, beads, chains), F32),), (*beads_in, planes, crossing, crossing_counts), (6,))
    below, above, picked = lax.optimization_barrier((below, above, picked))
    rise, sums, carry, fall = local_call(
        functools.partial(rise_kernel, *sizes), "rise_step",
        (((1, beads * chains), F32), ((blocks, rows, LANES), F32),
         ((blocks + 1, rows // 2, LANES), F32), ((extra, LANES), F32)),
        (((PIECES * ROWS, width), E4), [((width, HALF_GROUP * chains), E4)] * 2,
         [(((1 + PIECES) * ROWS, HALF_GROUP * chains), E4)] * 2, (((1 + PIECES) * ROWS, width), F32),
         ((beads, chains), F32)),
        (*beads_in, planes, below, above, crossing, crossing_counts, picked), (8,))
    carried, fallen = ring(carry, 1), ring(fall, -1)
    merged, = local_call(
        merge_kernel, "merge_step", (((blocks, rows, LANES), F32),), (), (sums, carried), limit=8)

    merged, base = lax.optimization_barrier((merged, base))
    parts = exchange(merged, halves)
    flat, = local_call(
        functools.partial(first_kernel, 0, FIRST_BEADS, layers, chains), "first_step",
        (((2, FIRST_BEADS * chains), F32),), (), (cells, split, base, table))
    parts, flat = lax.optimization_barrier((parts, flat))
    folded, = local_call(
        fold_kernel, "fold_step", (((2, rows // 2 + 2 * extra, LANES), F32),), (), (parts, carried, fallen), limit=8)
    folded, base = lax.optimization_barrier((folded, base))
    both = exchange(folded, pairs)
    new, = local_call(
        functools.partial(rest_kernel, FIRST_BEADS, beads, layers, chains), "rest_step",
        (((3, beads * chains), F32),), (), (cells, split, base, table, flat, rise))
    both, new = lax.optimization_barrier((both, new))
    density_scale = GRID * GRID * layers / (reps * chains * beads)
    density, arrived = local_call(
        functools.partial(last_kernel, layers, density_scale), "last_step",
        (((2, layers, CELLS // reps), F32), ((3, 2, chains), F32)), (), (both, carried, fallen, own), (3,), limit=8)
    return new, density, arrived.transpose(1, 0, 2)


def solution(mesh):
    in_specs = (
        P(None, ("dom", "rep")),
        P(None, ("dom", "rep")),
        P(None, ("dom", "rep")),
        P(("dom", "rep")),
        P(None, "dom", None),
        P(("dom", "rep"), None, None),
        P(("dom", "rep"), None),
    )
    out_specs = (P(None, ("dom", "rep")), P(None, "dom", "rep"), P(None, None, ("dom", "rep")))
    return jax.shard_map(shards, mesh=mesh, in_specs=in_specs, out_specs=out_specs, check_vma=False)
```
